32 devices in a mesh: row: 16 (over z, y, core), col: 2 (over x).
Axes of the slice: x: 2, y: 2, z: 4, core: 2. Of those that a mesh axis runs over, the one named last changes fastest.
Arguments:
- object_field: bfloat16 [2, 4096, 2048], P(None, 'row', 'col'), may hold values from -6 to 6
- probe: float32 [2, 2, 256, 256], replicated, may hold values from -5 to 5
- measured: bfloat16 [16, 2, 12, 256, 256], P('row', 'col'), may hold values from 0.3984375 to 4
- positions: int32 [16, 2, 12, 2], P('row', 'col'), may hold values from 0 to 1023, as said below
- counts: int32 [16, 2], P('row', 'col'), may hold values from 1 to 12, as said below
Outputs:
- object_grad: float32 [2, 4096, 2048], P(None, 'row', 'col')
- probe_grad: float32 [2, 2, 256, 256], replicated
The draws below stay inside these ranges and needn't reach their ends.
Inputs may be any that keep to these rules, and one draw needn't show every extreme that they name: positions[i, j, s, 0] lies in 0 to 255 and positions[i, j, s, 1] in 0 to 1023 for every slot, live or not. `counts`: some tile has all 12 slots live.
All inputs are finite; a program needn't handle non-finite values.
Results may differ from the reference program's by a relative error of at most 0.0048.
The reference program's roundings to bfloat16 on the way (of `patch`, `wave` and `weighted`) count: a program that leaves them out, or rounds other values in their place, can miss the bound.
Values may be sent and summed in bfloat16 or wider, within the bound.
A program may use at most 128 MiB of HBM per device.

```python
import math
import jax
import jax.numpy as jnp
from jax import lax

P_SIZE = 256
MODES = 2
TILE_R = 256
TILE_C = 1024
SLOTS = 12
GRID_R = 16
GRID_C = 2
OBJ_R = 4096
OBJ_C = 2048
N_ROW = 16
N_COL = 2


def draw_positions(key, part):
    key_rows = jax.random.fold_in(key, 11)
    key_cols = jax.random.fold_in(key, 12)
    rows = jax.random.randint(key_rows, (GRID_R, GRID_C, SLOTS, 1), 0, TILE_R)
    cols = jax.random.randint(key_cols, (GRID_R, GRID_C, SLOTS, 1), 0, TILE_C)
    return jnp.concatenate([rows, cols], 3).astype(jnp.int32)


def draw_counts(key, part):
    key_first = jax.random.fold_in(key, 21)
    key_second = jax.random.fold_in(key, 22)
    key_pick = jax.random.fold_in(key, 23)
    first = jax.random.randint(key_first, (GRID_R * GRID_C,), 0, SLOTS)
    second = jax.random.randint(key_second, (GRID_R * GRID_C,), 0, SLOTS)
    counts = 1 + first * second // (SLOTS - 1)
    chosen = jax.random.randint(key_pick, (), 0, GRID_R * GRID_C)
    counts = counts.at[chosen].set(SLOTS)
    return counts.reshape(GRID_R, GRID_C).astype(jnp.int32)


def block_levels(stream_key, shape, cuts, smallest, top_value):
    gain, own = 1.0, jax.random.fold_in(stream_key, 6)
    for position, blocks in cuts:
        steps = jnp.exp(jax.random.uniform(jax.random.fold_in(own, position), (blocks,), jnp.float32, smallest / len(cuts), top_value / len(cuts)))
        gain = gain * jnp.repeat(steps, shape[position] // blocks).reshape([-1 if axis == position else 1 for axis in range(len(shape))])
    return gain


def bell_draw(own_key, shape, deviation, limit, shards=(), held_as=jnp.bfloat16):
    values = jax.random.normal(own_key, shape, jnp.float32) * deviation
    if len(shards) > 0:
        values = block_levels(own_key, shape, shards, -0.22, 0.18) * values
    return jnp.clip(values, min=-limit, max=limit).astype(held_as)


def setup_inputs(seed: int = 0) -> dict:
    keys = jax.random.split(jax.random.key(seed), 6)
    object_field = bell_draw(keys[0], (2, OBJ_R, OBJ_C), 1.0, 6.0, ((1, 16), (2, 2)))
    probe = bell_draw(keys[1], (MODES, 2, P_SIZE, P_SIZE), 0.7, 5.0, (), jnp.float32)
    measured = jnp.clip(jnp.exp(math.log(4.0) - 2.306499 * jax.random.uniform(keys[2], (GRID_R, GRID_C, SLOTS, P_SIZE, P_SIZE), jnp.float32) ** block_levels(keys[2], (GRID_R, GRID_C, SLOTS, P_SIZE, P_SIZE), ((0, 16), (1, 2)), -0.2, 0.2)), 0.3984375, 4.0).astype(jnp.bfloat16)
    positions = draw_positions(jax.random.fold_in(keys[5], 71), 0)
    counts = draw_counts(jax.random.fold_in(keys[5], 71), 0)
    return dict(object_field=object_field, probe=probe, measured=measured, positions=positions, counts=counts)


def dft_tables(size, sign):
    index = jnp.arange(size, dtype=jnp.int32)
    phase = index[:, None] * index[None, :] % size
    angle = 2.0 * jnp.pi / size * phase.astype(jnp.float32)
    cosine = jnp.cos(angle) / jnp.sqrt(jnp.float32(size))
    sine = sign * jnp.sin(angle) / jnp.sqrt(jnp.float32(size))
    left = jnp.stack([jnp.stack([cosine, sine], 0), jnp.stack([-sine, cosine], 0)], 0)
    right = jnp.stack([jnp.stack([cosine, -sine], 1), jnp.stack([sine, cosine], 1)], 0)
    return (left.astype(jnp.bfloat16), right.astype(jnp.bfloat16))

def transform(field, left, right):
    half = jnp.einsum('ocij,mcjk->moik', left.astype(jnp.float32), field.astype(jnp.float32), precision=lax.Precision.HIGHEST)
    half = half.astype(jnp.bfloat16)
    return jnp.einsum('mcij,cjdk->mdik', half.astype(jnp.float32), right.astype(jnp.float32), precision=lax.Precision.HIGHEST)

def position_terms(patch, frame, probe, tables):
    fwd_left, fwd_right, inv_left, inv_right = tables
    obj = patch.astype(jnp.float32)
    obj_re, obj_im = (obj[0], obj[1])
    pro_re, pro_im = (probe[:, 0], probe[:, 1])
    wave = jnp.stack([pro_re * obj_re - pro_im * obj_im, pro_re * obj_im + pro_im * obj_re], 1).astype(jnp.bfloat16)
    spectrum = transform(wave, fwd_left, fwd_right)
    intensity = lax.optimization_barrier(jnp.sum(spectrum * spectrum, axis=(0, 1)))
    amplitude = jnp.sqrt(intensity + 1.0)
    factor = 1.0 - frame.astype(jnp.float32) / amplitude
    weighted = (spectrum * factor).astype(jnp.bfloat16)
    back = transform(weighted, inv_left, inv_right)
    back_re, back_im = (back[:, 0], back[:, 1])
    obj_grad = jnp.stack([lax.optimization_barrier(jnp.sum(pro_re * back_re + pro_im * back_im, 0)), lax.optimization_barrier(jnp.sum(pro_re * back_im - pro_im * back_re, 0))], 0)
    probe_part = jnp.stack([obj_re * back_re + obj_im * back_im, obj_re * back_im - obj_im * back_re], 1)
    return (obj_grad, probe_part)

def reference(object_field, probe, measured, positions, counts):
    fwd_left, fwd_right = dft_tables(P_SIZE, 1.0)
    inv_left, inv_right = dft_tables(P_SIZE, -1.0)
    tables = (fwd_left, fwd_right, inv_left, inv_right)
    padded = jnp.pad(object_field, ((0, 0), (0, P_SIZE), (0, P_SIZE)))
    grad = jnp.zeros(padded.shape, jnp.float32)
    probe_sum = jnp.zeros(probe.shape, jnp.float32)
    total = N_ROW * N_COL * SLOTS
    items = jnp.arange(total, dtype=jnp.int32)
    tile_r = items // (N_COL * SLOTS)
    tile_c = items // SLOTS % N_COL
    slot = items % SLOTS
    flat_pos = positions.reshape(total, 2).astype(jnp.int32)
    flat_counts = counts.reshape(N_ROW * N_COL).astype(jnp.int32)
    live = slot < flat_counts[items // SLOTS]
    start_r = (tile_r * TILE_R + flat_pos[:, 0]).astype(jnp.int32)
    start_c = (tile_c * TILE_C + flat_pos[:, 1]).astype(jnp.int32)
    flat_measured = measured.reshape(total, P_SIZE, P_SIZE)
    zero = jnp.zeros((), jnp.int32)

    def step(carry, item):
        index, row_at, col_at, alive = item

        def active(state):
            grad_now, probe_now = state
            patch = lax.dynamic_slice(padded, (zero, row_at, col_at), (2, P_SIZE, P_SIZE))
            obj_grad, probe_part = position_terms(patch, flat_measured[index], probe, tables)
            old = lax.dynamic_slice(grad_now, (zero, row_at, col_at), (2, P_SIZE, P_SIZE))
            grad_now = lax.dynamic_update_slice(grad_now, old + obj_grad, (zero, row_at, col_at))
            return (grad_now, probe_now + probe_part)
        return (lax.cond(alive, active, lambda state: state, carry), None)
    (grad, probe_sum), _ = lax.scan(step, (grad, probe_sum), (items, start_r, start_c, live))
    object_grad = grad[:, :TILE_R * N_ROW, :TILE_C * N_COL]
    probe_grad = probe_sum / jnp.sqrt(jnp.float32(total))
    return (object_grad, probe_grad)
```

```python
import functools

import jax
import jax.numpy as jnp
import numpy as np
from jax import lax
from jax.experimental import pallas as pl
from jax.experimental.pallas import tpu as pltpu
from jax.sharding import PartitionSpec as P

MESH = pl.DeviceIdType.MESH
LANES = 128
CHUNK = 64
F32 = jnp.float32
BF16 = jnp.bfloat16


def dft_blocks(size):
    index = np.arange(size)
    angle = 2.0 * np.pi / size * (index[:, None] * index[None, :] % size)
    cosine = np.cos(angle) / np.sqrt(size)
    sine = np.sin(angle) / np.sqrt(size)
    one = np.block([[cosine, sine], [-sine, cosine]])
    other = np.block([[cosine, -sine], [sine, cosine]])
    return jnp.asarray(one, F32).astype(BF16), jnp.asarray(other, F32).astype(BF16)


def dot(a, b):
    return jnp.dot(a, b, preferred_element_type=F32)


def work_kernel(
    pos_ref, count_ref, own_ref, below_ref, strip_ref, corner_ref, frames_ref, probe_ref, one_ref, other_ref,
    grad_ref, band_ref, side_ref, edge_ref, sum_ref,
    ext, acc, patch, wave, half, weighted, half2,
):
    rows, cols = own_ref.shape[1:]
    size = probe_ref.shape[-1]
    high, blocks = rows + size, (cols + size) // LANES

    def line(plane, block, row):
        return (plane * blocks + block) * high + row

    for c in range(2):
        for block in range(blocks):
            at = block * LANES
            inside = at < cols
            at = at if inside else at - cols
            top, bottom = (own_ref, below_ref) if inside else (strip_ref, corner_ref)
            ext[pl.ds(line(c, block, 0), rows), :] = top[c, :, at : at + LANES].astype(F32)
            ext[pl.ds(line(c, block, rows), size), :] = bottom[c, :, at : at + LANES].astype(F32)
    acc[...] = jnp.zeros_like(acc)
    sum_ref[...] = jnp.zeros_like(sum_ref)
    per = size // LANES
    lane = lax.broadcasted_iota(jnp.int32, (CHUNK, LANES), 1)

    @pl.loop(0, count_ref[0])
    def _(slot):
        row = pos_ref[2 * slot]
        col = pos_ref[2 * slot + 1]
        first = col // LANES
        shift = col - first * LANES
        back_shift = lax.rem(LANES - shift, LANES)
        low = lane < LANES - shift
        high_lanes = lane >= shift
        for start in range(0, size, CHUNK):
            rs = pl.ds(start, CHUNK)
            obj = []
            for c in range(2):
                turned = [
                    pltpu.roll(ext[pl.ds(line(c, first + b, row + start), CHUNK), :], back_shift, 1)
                    for b in range(per + 1)
                ]
                value = jnp.concatenate([jnp.where(low, turned[b], turned[b + 1]) for b in range(per)], 1)
                patch[c, rs, :] = value
                obj.append(value)
            re, im = obj
            for m in range(2):
                pre, pim = probe_ref[m, 0, rs, :], probe_ref[m, 1, rs, :]
                ms = pl.ds(m * size, size)
                wave[rs, ms] = (pre * re - pim * im).astype(BF16)
                wave[pl.ds(size + start, CHUNK), ms] = (pre * im + pim * re).astype(BF16)
        for o in range(2):
            os = pl.ds(o * size, size)
            out = dot(one_ref[os, :], wave[...])
            for m in range(2):
                half[pl.ds(m * size, size), os] = out[:, m * size : (m + 1) * size].astype(BF16)
        for start in range(0, size, 2 * CHUNK):
            spec = [dot(half[pl.ds(m * size + start, 2 * CHUNK), :], other_ref[...]) for m in range(2)]
            for sub in range(0, 2 * CHUNK, CHUNK):
                s = [v[sub : sub + CHUNK] for v in spec]
                square = [v[:, :size] * v[:, :size] + v[:, size:] * v[:, size:] for v in s]
                inv = lax.rsqrt(square[0] + square[1] + 1.0)
                rs = pl.ds(start + sub, CHUNK)
                factor = 1.0 - frames_ref[slot, rs, :].astype(F32) * inv
                for m in range(2):
                    for d in range(2):
                        part = s[m][:, d * size : (d + 1) * size] * factor
                        weighted[pl.ds(d * size + start + sub, CHUNK), pl.ds(m * size, size)] = part.astype(BF16)
        for o in range(2):
            os = pl.ds(o * size, size)
            out = dot(other_ref[os, :], weighted[...])
            for m in range(2):
                half2[pl.ds(m * size, size), os] = out[:, m * size : (m + 1) * size].astype(BF16)
        for start in range(0, size, 2 * CHUNK):
            back = [dot(half2[pl.ds(m * size + start, 2 * CHUNK), :], one_ref[...]) for m in range(2)]
            for sub in range(0, 2 * CHUNK, CHUNK):
                at = start + sub
                rs = pl.ds(at, CHUNK)
                ore, oim = patch[0, rs, :], patch[1, rs, :]
                gre = gim = None
                for m in range(2):
                    bre = back[m][sub : sub + CHUNK, :size]
                    bim = back[m][sub : sub + CHUNK, size:]
                    pre, pim = probe_ref[m, 0, rs, :], probe_ref[m, 1, rs, :]
                    a = pre * bre + pim * bim
                    b = pre * bim - pim * bre
                    gre, gim = (a, b) if m == 0 else (gre + a, gim + b)
                    qre = ore * bre + oim * bim
                    qim = ore * bim - oim * bre
                    for d, q in enumerate((qre, qim)):
                        for h in range(size // LANES):
                            block = (m * 2 + d) * (size // LANES) + h
                            sum_ref[pl.ds(block * size + at, CHUNK), :] += q[:, h * LANES : (h + 1) * LANES]
                nothing = jnp.zeros((CHUNK, LANES), F32)
                for c, g in enumerate((gre, gim)):
                    turned = [pltpu.roll(g[:, b * LANES : (b + 1) * LANES], shift, 1) for b in range(per)]
                    turned = [nothing] + turned + [nothing]
                    for b in range(per + 1):
                        here = pl.ds(line(c, first + b, row + at), CHUNK)
                        acc[here, :] += jnp.where(high_lanes, turned[b + 1], turned[b])

    for c in range(2):
        for block in range(blocks):
            at = block * LANES
            inside = at < cols
            at = at if inside else at - cols
            upper = acc[pl.ds(line(c, block, 0), rows), :]
            lower = acc[pl.ds(line(c, block, rows), size), :].astype(BF16)
            if inside:
                grad_ref[c, :, at : at + LANES] = upper
                band_ref[c, :, at : at + LANES] = lower
            else:
                side_ref[c, :, at : at + LANES] = upper.astype(BF16)
                edge_ref[c, :, at : at + LANES] = lower


def join_kernel(
    n_row, n_col, scale,
    grad_ref, band_ref, side_ref, edge_ref, sum_ref,
    out_ref, probe_ref,
    band_in, side_in, edge_in, send1, recv1, acc, send2, recv2, acc2, recv3, full2, full1, wide, send_sem, recv_sem,
):
    i, j = lax.axis_index("row"), lax.axis_index("col")
    size2, size3 = 2 * n_col, n_row // 4
    k = lax.rem(i, 2)
    g2 = lax.rem(i // 2, 2) * n_col + j
    g3 = i // 4
    n1 = sum_ref.shape[0] // 2
    n2 = n1 // size2
    n3 = n2 // size3
    partner = (i + 1 - 2 * k, j)

    def peer2(d):
        p = lax.rem(g2 + d, size2)
        return (g3 * 4 + p // n_col * 2 + k, lax.rem(p, n_col))

    def peer3(d):
        return (lax.rem(g3 + d, size3) * 4 + lax.rem(i, 4), j)

    has_down, has_up, has_right, has_left = i < n_row - 1, i > 0, j < n_col - 1, j > 0
    sides = (
        (has_down, has_up, (i + 1, j), (i - 1, j), band_ref, band_in),
        (has_right, has_left, (i, j + 1), (i, j - 1), side_ref, side_in),
        (has_down & has_right, has_up & has_left, (i + 1, j + 1), (i - 1, j - 1), edge_ref, edge_in),
    )
    barrier = pltpu.get_barrier_semaphore()
    peers = [partner] + [peer2(d) for d in range(1, size2)] + [peer3(d) for d in range(1, size3)]
    for peer in peers:
        pl.semaphore_signal(barrier, inc=1, device_id=peer, device_id_type=MESH)
    for _, gets, _, source, _, _ in sides:

        @pl.when(gets)
        def _():
            pl.semaphore_signal(barrier, inc=1, device_id=source, device_id_type=MESH)

    targets = sum(sends.astype(jnp.int32) for sends, _, _, _, _, _ in sides)
    pl.semaphore_wait(barrier, len(peers) + targets)

    used = [0]

    def copy(src, dst, to):
        at = used[0]
        used[0] += 1
        return pltpu.make_async_remote_copy(
            src_ref=src, dst_ref=dst, send_sem=send_sem.at[at], recv_sem=recv_sem.at[at], device_id=to, device_id_type=MESH
        )

    send1[...] = sum_ref[pl.ds(pl.multiple_of((1 - k) * n1, n1), n1), :].astype(BF16)
    first = copy(send1, recv1, partner)
    first.start()
    side_copies = []
    for sends, gets, to, _, src, dst in sides:
        c = copy(src, dst, to)
        side_copies.append(c)

        @pl.when(sends)
        def _():
            c.start()

    first.wait()
    total = sum_ref[pl.ds(pl.multiple_of(k * n1, n1), n1), :] + recv1[...].astype(F32)
    acc[...] = total
    send2[...] = total.astype(BF16).reshape(send2.shape)
    second = [copy(send2.at[lax.rem(g2 + d, size2)], recv2.at[d - 1], peer2(d)) for d in range(1, size2)]
    for c in second:
        c.start()
    total = acc[pl.ds(pl.multiple_of(g2 * n2, n2), n2), :]
    for d, c in enumerate(second):
        c.wait()
        total = total + recv2[d].astype(F32)
    acc2[...] = total.reshape(acc2.shape)
    third = [copy(acc2.at[lax.rem(g3 + d, size3)], recv3.at[d - 1], peer3(d)) for d in range(1, size3)]
    for c in third:
        c.start()
    total = acc2[g3]
    for d, c in enumerate(third):
        c.wait()
        total = total + recv3[d]
    full2[g3] = total * scale
    third = [copy(full2.at[g3], full2.at[g3], peer3(d)) for d in range(1, size3)]
    for c in third:
        c.start()
    for c in third:
        c.wait()
    full1[g2] = full2[...].reshape(n2, LANES).astype(BF16)
    second = [copy(full1.at[g2], full1.at[g2], peer2(d)) for d in range(1, size2)]
    for c in second:
        c.start()
    for c in second:
        c.wait()
    wide[k] = full1[...].reshape(n1, LANES)
    last = copy(wide.at[k], wide.at[k], partner)
    last.start()
    out_ref[...] = grad_ref[...]
    rows, cols = out_ref.shape[1:]
    size = probe_ref.shape[-1]
    for (sends, gets, _, _, _, dst), c in zip(sides, side_copies):
        span = dst.shape[2]

        @pl.when(gets)
        def _():
            c.wait_recv()
            out_ref[:, :, :span] += dst[...].astype(F32)

        @pl.when(sends)
        def _():
            c.wait_send()

    last.wait()
    per = size // LANES
    for block in range(4 * per):
        part = wide[block * size // n1, pl.ds(block * size % n1, size), :]
        mode, plane, h = block // (2 * per), block // per % 2, block % per
        probe_ref[mode, plane, :, h * LANES : (h + 1) * LANES] = part.astype(F32)


def body(n_row, n_col, object_field, probe, measured, positions, counts):
    size = probe.shape[-1]
    rows, cols = object_field.shape[1:]
    slots = measured.shape[2]
    one, other = dft_blocks(size)
    head = object_field[:, :, :size]
    below = lax.ppermute(object_field, "row", [(i + 1, i) for i in range(n_row - 1)])
    strip = lax.ppermute(head, "col", [(j + 1, j) for j in range(n_col - 1)])
    diagonal = [
        ((i + 1) * n_col + j + 1, i * n_col + j) for i in range(n_row - 1) for j in range(n_col - 1)
    ]
    corner = lax.ppermute(head, ("row", "col"), diagonal)
    vmem = pl.BlockSpec(memory_space=pltpu.VMEM)
    smem = pl.BlockSpec(memory_space=pltpu.SMEM)
    lines = 4 * size * size // LANES
    work = pl.pallas_call(
        work_kernel,
        out_shape=[
            jax.ShapeDtypeStruct((2, rows, cols), F32),
            jax.ShapeDtypeStruct((2, size, cols), BF16),
            jax.ShapeDtypeStruct((2, rows, size), BF16),
            jax.ShapeDtypeStruct((2, size, size), BF16),
            jax.ShapeDtypeStruct((lines, LANES), F32),
        ],
        in_specs=[smem, smem] + [vmem] * 8,
        out_specs=[vmem] * 5,
        scratch_shapes=[
            pltpu.VMEM((2 * (rows + size) * (cols + size) // LANES, LANES), F32),
            pltpu.VMEM((2 * (rows + size) * (cols + size) // LANES, LANES), F32),
            pltpu.VMEM((2, size, size), F32),
        ]
        + [pltpu.VMEM((2 * size, 2 * size), BF16)] * 4,
        compiler_params=pltpu.CompilerParams(vmem_limit_bytes=48 * 2**20),
        name="scan",
    )
    grad, band, side, edge, total = work(
        positions.reshape(-1), counts.reshape(-1), object_field, below, strip, corner, measured[0, 0], probe, one, other
    )
    size2, size3 = 2 * n_col, n_row // 4
    n1 = lines // 2
    n2 = n1 // size2
    n3 = n2 // size3
    n_copies = 2 + 3 + 2 * (size2 - 1) + 2 * (size3 - 1)
    join = pl.pallas_call(
        functools.partial(join_kernel, n_row, n_col, 1.0 / float(np.sqrt(slots * n_row * n_col))),
        out_shape=[
            jax.ShapeDtypeStruct((2, rows, cols), F32),
            jax.ShapeDtypeStruct(probe.shape, F32),
        ],
        in_specs=[vmem] * 5,
        out_specs=[vmem] * 2,
        scratch_shapes=[
            pltpu.VMEM(band.shape, BF16),
            pltpu.VMEM(side.shape, BF16),
            pltpu.VMEM(edge.shape, BF16),
            pltpu.VMEM((n1, LANES), BF16),
            pltpu.VMEM((n1, LANES), BF16),
            pltpu.VMEM((n1, LANES), F32),
            pltpu.VMEM((size2, n2, LANES), BF16),
            pltpu.VMEM((size2 - 1, n2, LANES), BF16),
            pltpu.VMEM((size3, n3, LANES), F32),
            pltpu.VMEM((size3 - 1, n3, LANES), F32),
            pltpu.VMEM((size3, n3, LANES), F32),
            pltpu.VMEM((size2, n2, LANES), BF16),
            pltpu.VMEM((2, n1, LANES), BF16),
            pltpu.SemaphoreType.DMA((n_copies,)),
            pltpu.SemaphoreType.DMA((n_copies,)),
        ],
        compiler_params=pltpu.CompilerParams(
            collective_id=0, has_side_effects=True, vmem_limit_bytes=40 * 2**20
        ),
        name="join",
    )
    return tuple(join(grad, band, side, edge, total))


def solution(mesh):
    placed = (
        P(None, "row", "col"),
        P(),
        P("row", "col", None, None, None),
        P("row", "col", None, None),
        P("row", "col"),
    )
    return jax.shard_map(
        functools.partial(body, mesh.shape["row"], mesh.shape["col"]),
        mesh=mesh,
        in_specs=placed,
        out_specs=(P(None, "row", "col"), P()),
        check_vma=False,
    )
```

```python
import functools

import jax
import jax.numpy as jnp
import numpy as np
from jax import lax
from jax.experimental import pallas as pl
from jax.experimental.pallas import tpu as pltpu
from jax.sharding import PartitionSpec as P

MESH = pl.DeviceIdType.MESH
LANES = 128
CHUNK = 64
F32 = jnp.float32
BF16 = jnp.bfloat16


def dft_blocks(size):
    index = np.arange(size)
    angle = 2.0 * np.pi / size * (index[:, None] * index[None, :] % size)
    cosine = np.cos(angle) / np.sqrt(size)
    sine = np.sin(angle) / np.sqrt(size)
    one = np.block([[cosine, sine], [-sine, cosine]])
    other = np.block([[cosine, -sine], [sine, cosine]])
    return jnp.asarray(one, F32).astype(BF16), jnp.asarray(other, F32).astype(BF16)


def dot(a, b):
    return jnp.dot(a, b, preferred_element_type=F32)


def work_kernel(
    pos_ref, count_ref, own_ref, below_ref, strip_ref, corner_ref, frames_ref, probe_ref, one_ref, other_ref,
    grad_ref, band_ref, side_ref, edge_ref, sum_ref,
    ext, acc, patch_all, wave_all, half_all, weighted_all, half2_all,
):
    rows, cols = own_ref.shape[1:]
    size = probe_ref.shape[-1]
    high, blocks = rows + size, (cols + size) // LANES

    def line(plane, block, row):
        return (plane * blocks + block) * high + row

    for c in range(2):
        for block in range(blocks):
            at = block * LANES
            inside = at < cols
            at = at if inside else at - cols
            top, bottom = (own_ref, below_ref) if inside else (strip_ref, corner_ref)
            ext[pl.ds(line(c, block, 0), rows), :] = top[c, :, at : at + LANES].astype(F32)
            ext[pl.ds(line(c, block, rows), size), :] = bottom[c, :, at : at + LANES].astype(F32)
    acc[...] = jnp.zeros_like(acc)
    sum_ref[...] = jnp.zeros_like(sum_ref)
    per = size // LANES
    lane = lax.broadcasted_iota(jnp.int32, (CHUNK, LANES), 1)

    bufs = [tuple(ref.at[t] for ref in (patch_all, wave_all, half_all, weighted_all, half2_all)) for t in range(2)]

    def place(slot):
        row = pos_ref[2 * slot]
        col = pos_ref[2 * slot + 1]
        first = col // LANES
        shift = col - first * LANES
        back_shift = lax.rem(LANES - shift, LANES)
        low = lane < LANES - shift
        high_lanes = lane >= shift
        return row, first, shift, back_shift, low, high_lanes

    def enter(at, patch, wave):
        row, first, shift, back_shift, low, high_lanes = at
        for start in range(0, size, CHUNK):
            rs = pl.ds(start, CHUNK)
            obj = []
            for c in range(2):
                turned = [
                    pltpu.roll(ext[pl.ds(line(c, first + b, row + start), CHUNK), :], back_shift, 1)
                    for b in range(per + 1)
                ]
                value = jnp.concatenate([jnp.where(low, turned[b], turned[b + 1]) for b in range(per)], 1)
                patch[c, rs, :] = value
                obj.append(value)
            re, im = obj
            for m in range(2):
                pre, pim = probe_ref[m, 0, rs, :], probe_ref[m, 1, rs, :]
                ms = pl.ds(m * size, size)
                wave[rs, ms] = (pre * re - pim * im).astype(BF16)
                wave[pl.ds(size + start, CHUNK), ms] = (pre * im + pim * re).astype(BF16)

    def left_one(wave, half):
        for o in range(2):
            os = pl.ds(o * size, size)
            out = dot(one_ref[os, :], wave[...])
            for m in range(2):
                half[pl.ds(m * size, size), os] = out[:, m * size : (m + 1) * size].astype(BF16)

    def weigh(slot, live, half, weighted):
        for start in range(0, size, 2 * CHUNK):
            spec = [dot(half[pl.ds(m * size + start, 2 * CHUNK), :], other_ref[...]) for m in range(2)]
            for sub in range(0, 2 * CHUNK, CHUNK):
                s = [v[sub : sub + CHUNK] for v in spec]
                square = [v[:, :size] * v[:, :size] + v[:, size:] * v[:, size:] for v in s]
                inv = lax.rsqrt(square[0] + square[1] + 1.0)
                rs = pl.ds(start + sub, CHUNK)
                factor = live * (1.0 - frames_ref[slot, rs, :].astype(F32) * inv)
                for m in range(2):
                    for d in range(2):
                        part = s[m][:, d * size : (d + 1) * size] * factor
                        weighted[pl.ds(d * size + start + sub, CHUNK), pl.ds(m * size, size)] = part.astype(BF16)

    def left_other(weighted, half2):
        for o in range(2):
            os = pl.ds(o * size, size)
            out = dot(other_ref[os, :], weighted[...])
            for m in range(2):
                half2[pl.ds(m * size, size), os] = out[:, m * size : (m + 1) * size].astype(BF16)

    def leave(spot, patch, half2):
        row, first, shift, back_shift, low, high_lanes = spot
        for start in range(0, size, 2 * CHUNK):
            back = [dot(half2[pl.ds(m * size + start, 2 * CHUNK), :], one_ref[...]) for m in range(2)]
            for sub in range(0, 2 * CHUNK, CHUNK):
                at = start + sub
                rs = pl.ds(at, CHUNK)
                ore, oim = patch[0, rs, :], patch[1, rs, :]
                gre = gim = None
                for m in range(2):
                    bre = back[m][sub : sub + CHUNK, :size]
                    bim = back[m][sub : sub + CHUNK, size:]
                    pre, pim = probe_ref[m, 0, rs, :], probe_ref[m, 1, rs, :]
                    a = pre * bre + pim * bim
                    b = pre * bim - pim * bre
                    gre, gim = (a, b) if m == 0 else (gre + a, gim + b)
                    qre = ore * bre + oim * bim
                    qim = ore * bim - oim * bre
                    for d, q in enumerate((qre, qim)):
                        for h in range(size // LANES):
                            block = (m * 2 + d) * (size // LANES) + h
                            sum_ref[pl.ds(block * size + at, CHUNK), :] += q[:, h * LANES : (h + 1) * LANES]
                nothing = jnp.zeros((CHUNK, LANES), F32)
                for c, g in enumerate((gre, gim)):
                    turned = [pltpu.roll(g[:, b * LANES : (b + 1) * LANES], shift, 1) for b in range(per)]
                    turned = [nothing] + turned + [nothing]
                    for b in range(per + 1):
                        here = pl.ds(line(c, first + b, row + at), CHUNK)
                        acc[here, :] += jnp.where(high_lanes, turned[b + 1], turned[b])

    slots = frames_ref.shape[0]
    count = count_ref[0]

    @pl.loop(0, (count + 1) // 2)
    def _(step):
        which = [2 * step, jnp.minimum(2 * step + 1, slots - 1)]
        alive = [jnp.float32(1.0), (2 * step + 1 < count).astype(F32)]
        spots = [place(slot) for slot in which]
        for t in range(2):
            patch, wave, half, weighted, half2 = bufs[t]
            enter(spots[t], patch, wave)
            left_one(wave, half)
        for t in range(2):
            patch, wave, half, weighted, half2 = bufs[t]
            weigh(which[t], alive[t], half, weighted)
            left_other(weighted, half2)
        for t in range(2):
            patch, wave, half, weighted, half2 = bufs[t]
            leave(spots[t], patch, half2)

    for c in range(2):
        for block in range(blocks):
            at = block * LANES
            inside = at < cols
            at = at if inside else at - cols
            upper = acc[pl.ds(line(c, block, 0), rows), :]
            lower = acc[pl.ds(line(c, block, rows), size), :].astype(BF16)
            if inside:
                grad_ref[c, :, at : at + LANES] = upper
                band_ref[c, :, at : at + LANES] = lower
            else:
                side_ref[c, :, at : at + LANES] = upper.astype(BF16)
                edge_ref[c, :, at : at + LANES] = lower


def fetch_kernel(n_row, n_col, own_ref, *refs):
    local_in, (below_ref, strip_ref, corner_ref) = refs[:4], refs[4:7]
    own_out, local_out = refs[7], refs[8:12]
    send_sem, recv_sem, local_sem = refs[12:]
    i, j = lax.axis_index("row"), lax.axis_index("col")
    size = strip_ref.shape[2]
    up, down, left, right = i > 0, i < n_row - 1, j > 0, j < n_col - 1
    local = [
        pltpu.make_async_copy(src, dst, local_sem.at[at])
        for at, (src, dst) in enumerate(zip((own_ref,) + tuple(local_in), (own_out,) + tuple(local_out)))
    ]
    barrier = pltpu.get_barrier_semaphore()

    @pl.when(right)
    def _():
        pl.semaphore_signal(barrier, inc=1, device_id=(i, j + 1), device_id_type=MESH)

    @pl.when(down)
    def _():
        pl.semaphore_signal(barrier, inc=1, device_id=(i + 1, j), device_id_type=MESH)

    @pl.when(left | up)
    def _():
        pl.semaphore_wait(barrier, left.astype(jnp.int32) + up.astype(jnp.int32))

    def copy(at, src, dst, to):
        return pltpu.make_async_remote_copy(
            src_ref=src, dst_ref=dst, send_sem=send_sem.at[at], recv_sem=recv_sem.at[at], device_id=to, device_id_type=MESH
        )

    side = copy(0, own_ref.at[:, :, pl.ds(0, size)], strip_ref, (i, j - 1))
    band = copy(1, own_ref, below_ref, (i - 1, j))
    edge = copy(2, strip_ref, corner_ref, (i - 1, j))
    pl.when(left)(side.start)
    pl.when(up)(band.start)
    for c in local:
        c.start()

    def blank(ref):
        def fill():
            ref[...] = jnp.zeros_like(ref)

        return fill

    pl.when(jnp.logical_not(right))(blank(strip_ref))
    pl.when(jnp.logical_not(right & down))(blank(corner_ref))
    pl.when(jnp.logical_not(down))(blank(below_ref))
    pl.when(right)(side.wait_recv)
    pl.when(right & up)(edge.start)
    for c in local:
        c.wait()
    pl.when(down)(band.wait_recv)
    pl.when(right & down)(edge.wait_recv)
    pl.when(left)(side.wait_send)
    pl.when(up)(band.wait_send)
    pl.when(right & up)(edge.wait_send)


def join_kernel(
    n_row, n_col, scale,
    grad_ref, band_ref, side_ref, edge_ref, sum_ref,
    out_ref, probe_ref,
    band_in, side_in, edge_in, side_sum, local_sem, send1, recv1, acc, send2, recv2, acc2, recv3, full2, full1, wide, send_sem, recv_sem,
):
    i, j = lax.axis_index("row"), lax.axis_index("col")
    size2, size3 = 2 * n_col, n_row // 4
    k = lax.rem(i, 2)
    g2 = lax.rem(i // 2, 2) * n_col + j
    g3 = i // 4
    n1 = sum_ref.shape[0] // 2
    n2 = n1 // size2
    n3 = n2 // size3
    partner = (i + 1 - 2 * k, j)

    def peer2(d):
        p = lax.rem(g2 + d, size2)
        return (g3 * 4 + p // n_col * 2 + k, lax.rem(p, n_col))

    def peer3(d):
        return (lax.rem(g3 + d, size3) * 4 + lax.rem(i, 4), j)

    has_down, has_up, has_right, has_left = i < n_row - 1, i > 0, j < n_col - 1, j > 0
    down = (i + 1, j)
    barrier = pltpu.get_barrier_semaphore()
    peers = [partner] + [peer2(d) for d in range(1, size2)] + [peer3(d) for d in range(1, size3)]
    for peer in peers:
        pl.semaphore_signal(barrier, inc=1, device_id=peer, device_id_type=MESH)

    @pl.when(has_up)
    def _():
        pl.semaphore_signal(barrier, inc=1, device_id=(i - 1, j), device_id_type=MESH)

    @pl.when(has_left)
    def _():
        pl.semaphore_signal(barrier, inc=1, device_id=(i, j - 1), device_id_type=MESH)

    start = pltpu.make_async_copy(grad_ref, out_ref, local_sem.at[0])
    start.start()
    pl.semaphore_wait(barrier, len(peers) + has_down.astype(jnp.int32) + has_right.astype(jnp.int32))

    used = [0]

    def copy(src, dst, to):
        at = used[0]
        used[0] += 1
        return pltpu.make_async_remote_copy(
            src_ref=src, dst_ref=dst, send_sem=send_sem.at[at], recv_sem=recv_sem.at[at], device_id=to, device_id_type=MESH
        )

    send1[...] = sum_ref[pl.ds(pl.multiple_of((1 - k) * n1, n1), n1), :].astype(BF16)
    first = copy(send1, recv1, partner)
    first.start()
    edge = copy(edge_ref, edge_in, down)
    side = copy(side_sum, side_in, (i, j + 1))
    bands = []
    for at in range(0, band_ref.shape[2], LANES):
        cut = (slice(None), slice(None), pl.ds(at, LANES))
        bands.append(copy(band_ref.at[cut], band_in.at[cut], down))
    waiting = list(bands)

    def release(n):
        for _ in range(min(n, len(waiting))):
            pl.when(has_down)(waiting.pop(0).start)

    pl.when(has_down & has_right)(edge.start)
    release(1)
    first.wait()
    total = sum_ref[pl.ds(pl.multiple_of(k * n1, n1), n1), :] + recv1[...].astype(F32)
    acc[...] = total
    send2[...] = total.astype(BF16).reshape(send2.shape)
    second = [copy(send2.at[lax.rem(g2 + d, size2)], recv2.at[d - 1], peer2(d)) for d in range(1, size2)]
    for c in second:
        c.start()
    release(1)
    total = acc[pl.ds(pl.multiple_of(g2 * n2, n2), n2), :]
    for d, c in enumerate(second):
        c.wait()
        total = total + recv2[d].astype(F32)
    acc2[...] = total.reshape(acc2.shape)
    third = [copy(acc2.at[lax.rem(g3 + d, size3)], recv3.at[d - 1], peer3(d)) for d in range(1, size3)]
    for c in third:
        c.start()
    release(2)

    @pl.when(has_up & has_right)
    def _():
        edge.wait_recv()
        side_sum[...] = (side_ref[...].astype(F32) + edge_in[...].astype(F32)).astype(BF16)

    @pl.when(has_right & jnp.logical_not(has_up))
    def _():
        side_sum[...] = side_ref[...]

    pl.when(has_right)(side.start)
    total = acc2[g3]
    for d, c in enumerate(third):
        c.wait()
        total = total + recv3[d]
    full2[g3] = total * scale
    third = [copy(full2.at[g3], full2.at[g3], peer3(d)) for d in range(1, size3)]
    for c in third:
        c.start()
    release(2)
    for c in third:
        c.wait()
    full1[g2] = full2[...].reshape(n2, LANES).astype(BF16)
    second = [copy(full1.at[g2], full1.at[g2], peer2(d)) for d in range(1, size2)]
    for c in second:
        c.start()
    release(len(waiting))
    for c in second:
        c.wait()
    wide[k] = full1[...].reshape(n1, LANES)
    last = copy(wide.at[k], wide.at[k], partner)
    last.start()
    size = probe_ref.shape[-1]
    start.wait()

    @pl.when(has_left)
    def _():
        side.wait_recv()
        out_ref[:, :, :size] += side_in[...].astype(F32)

    @pl.when(has_up)
    def _():
        for at, c in enumerate(bands):
            c.wait_recv()
            span = pl.ds(at * LANES, LANES)
            out_ref[:, :, span] += band_in[:, :, span].astype(F32)

    @pl.when(has_right)
    def _():
        side.wait_send()

    @pl.when(has_down)
    def _():
        for c in bands:
            c.wait_send()

    pl.when(has_down & has_right)(edge.wait_send)
    last.wait()
    per = size // LANES
    for block in range(4 * per):
        part = wide[block * size // n1, pl.ds(block * size % n1, size), :]
        mode, plane, h = block // (2 * per), block // per % 2, block % per
        probe_ref[mode, plane, :, h * LANES : (h + 1) * LANES] = part.astype(F32)


def body(n_row, n_col, object_field, probe, measured, positions, counts):
    size = probe.shape[-1]
    rows, cols = object_field.shape[1:]
    slots = measured.shape[2]
    one, other = dft_blocks(size)
    vmem = pl.BlockSpec(memory_space=pltpu.VMEM)
    smem = pl.BlockSpec(memory_space=pltpu.SMEM)
    anywhere = pl.BlockSpec(memory_space=pl.ANY)
    local = (measured[0, 0], probe, one, other)
    below, strip, corner, own, frames, probe_near, one_near, other_near = pl.pallas_call(
        functools.partial(fetch_kernel, n_row, n_col),
        out_shape=[
            jax.ShapeDtypeStruct((2, size, cols), BF16),
            jax.ShapeDtypeStruct((2, rows, size), BF16),
            jax.ShapeDtypeStruct((2, size, size), BF16),
        ]
        + [jax.ShapeDtypeStruct(x.shape, x.dtype) for x in (object_field,) + local],
        in_specs=[pl.BlockSpec(memory_space=pltpu.HBM)] * 5,
        out_specs=[vmem] * 8,
        scratch_shapes=[
            pltpu.SemaphoreType.DMA((3,)),
            pltpu.SemaphoreType.DMA((3,)),
            pltpu.SemaphoreType.DMA((5,)),
        ],
        compiler_params=pltpu.CompilerParams(
            collective_id=1, has_side_effects=True, vmem_limit_bytes=44 * 2**20
        ),
        name="fetch",
    )(object_field, *local)
    lines = 4 * size * size // LANES
    work = pl.pallas_call(
        work_kernel,
        out_shape=[
            jax.ShapeDtypeStruct((2, rows, cols), F32),
            jax.ShapeDtypeStruct((2, size, cols), BF16),
            jax.ShapeDtypeStruct((2, rows, size), BF16),
            jax.ShapeDtypeStruct((2, size, size), BF16),
            jax.ShapeDtypeStruct((lines, LANES), F32),
        ],
        in_specs=[smem, smem] + [vmem] * 8,
        out_specs=[vmem] * 5,
        scratch_shapes=[
            pltpu.VMEM((2 * (rows + size) * (cols + size) // LANES, LANES), F32),
            pltpu.VMEM((2 * (rows + size) * (cols + size) // LANES, LANES), F32),
            pltpu.VMEM((2, 2, size, size), F32),
        ]
        + [pltpu.VMEM((2, 2 * size, 2 * size), BF16)] * 4,
        compiler_params=pltpu.CompilerParams(vmem_limit_bytes=30 * 2**20),
        name="scan",
    )
    grad, band, side, edge, total = work(
        positions.reshape(-1), counts.reshape(-1), own, below, strip, corner, frames, probe_near, one_near, other_near
    )
    size2, size3 = 2 * n_col, n_row // 4
    n1 = lines // 2
    n2 = n1 // size2
    n3 = n2 // size3
    n_copies = 2 + 2 + cols // LANES + 2 * (size2 - 1) + 2 * (size3 - 1)
    join = pl.pallas_call(
        functools.partial(join_kernel, n_row, n_col, 1.0 / float(np.sqrt(slots * n_row * n_col))),
        out_shape=[
            jax.ShapeDtypeStruct((2, rows, cols), F32),
            jax.ShapeDtypeStruct(probe.shape, F32),
        ],
        in_specs=[anywhere] + [vmem] * 4,
        out_specs=[vmem] * 2,
        scratch_shapes=[
            pltpu.VMEM(band.shape, BF16),
            pltpu.VMEM(side.shape, BF16),
            pltpu.VMEM(edge.shape, BF16),
            pltpu.VMEM(side.shape, BF16),
            pltpu.SemaphoreType.DMA((1,)),
            pltpu.VMEM((n1, LANES), BF16),
            pltpu.VMEM((n1, LANES), BF16),
            pltpu.VMEM((n1, LANES), F32),
            pltpu.VMEM((size2, n2, LANES), BF16),
            pltpu.VMEM((size2 - 1, n2, LANES), BF16),
            pltpu.VMEM((size3, n3, LANES), F32),
            pltpu.VMEM((size3 - 1, n3, LANES), F32),
            pltpu.VMEM((size3, n3, LANES), F32),
            pltpu.VMEM((size2, n2, LANES), BF16),
            pltpu.VMEM((2, n1, LANES), BF16),
            pltpu.SemaphoreType.DMA((n_copies,)),
            pltpu.SemaphoreType.DMA((n_copies,)),
        ],
        compiler_params=pltpu.CompilerParams(
            collective_id=0, has_side_effects=True, vmem_limit_bytes=18 * 2**20
        ),
        name="join",
    )
    return tuple(join(grad, band, side, edge, total))


def solution(mesh):
    placed = (
        P(None, "row", "col"),
        P(),
        P("row", "col", None, None, None),
        P("row", "col", None, None),
        P("row", "col"),
    )
    return jax.shard_map(
        functools.partial(body, mesh.shape["row"], mesh.shape["col"]),
        mesh=mesh,
        in_specs=placed,
        out_specs=(P(None, "row", "col"), P()),
        check_vma=False,
    )
```
